256 devices in a mesh: row: 16 (over z, x_lo), col: 16 (over y, x_hi, core).
Axes of the slice: x: 4 (x_hi: 2, x_lo: 2; x = x_hi * 2 + x_lo), y: 4, z: 8, core: 2. Of those that a mesh axis runs over, the one named last changes fastest.
Arguments:
- tokens: bfloat16 [512, 12288], P('col', 'row'), may hold values from -6 to 6
- up_weight: bfloat16 [12288, 24576], P('row', 'col'), may hold values from -0.0546875 to 0.0546875
- down_weight: bfloat16 [24576, 12288], P('col', 'row'), may hold values from -0.0390625 to 0.0390625
- out_grad: bfloat16 [512, 12288], P('col', 'row'), may hold values from -6 to 6
Outputs:
- output: bfloat16 [512, 12288], P('col', 'row')
- token_grad: bfloat16 [512, 12288], P('col', 'row')
- up_grad: bfloat16 [12288, 24576], P('row', 'col')
- down_grad: bfloat16 [24576, 12288], P('col', 'row')
The draws below stay inside these ranges and needn't reach their ends.
All inputs are finite; a program needn't handle non-finite values.
Results may differ from the reference program's by a relative error of at most 0.005.
Values may be sent and summed in bfloat16 or wider, within the bound.
No kernel may reach another device: no remote copies, remote signals or barrier semaphores. Data moves between devices by JAX's collectives and lax.ppermute only.
A program may use at most 64 MiB of HBM per device.

```python
import math
import jax
import jax.numpy as jnp

D = 12288
FF = 24576
TOKENS = 512


def levels(rng, dims, shards, least, top_value):
    factor_of = 1.0
    for axis_at, blocks in shards:
        steps = jax.random.uniform(jax.random.fold_in(jax.random.fold_in(rng, 6), axis_at), (blocks,), jnp.float32, least / len(shards), top_value / len(shards))
        factor_of = factor_of * jnp.repeat(jnp.exp(steps), dims[axis_at] // blocks).reshape((-1,) + (1,) * (len(dims) - 1 - axis_at))
    return factor_of


def scatter_about(stream_key, extent, width, reach, cuts=(), dtype=jnp.bfloat16):
    entries = width * jax.random.normal(stream_key, extent, jnp.float32)
    if cuts:
        entries = entries * levels(stream_key, extent, cuts, -0.22, 0.18)
    return jnp.clip(entries, -reach, reach).astype(dtype)


def setup_inputs(seed: int = 0) -> dict:
    arg_keys = jax.random.split(jax.random.key(seed), 5)
    tokens = scatter_about(arg_keys[0], (TOKENS, D), 1.0, 6.0, ((0, 16), (1, 16)))
    up_weight = scatter_about(arg_keys[1], (D, FF), D ** -0.5, 0.0546875, ((0, 16), (1, 16)))
    down_weight = scatter_about(arg_keys[2], (FF, D), FF ** -0.5, 0.0390625, ((0, 16), (1, 16)))
    out_grad = scatter_about(arg_keys[3], (TOKENS, D), 1.0, 6.0, ((0, 16), (1, 16)))
    return dict(tokens=tokens, up_weight=up_weight, down_weight=down_weight, out_grad=out_grad)


tanh_scale = math.sqrt(2.0 / math.pi)

def gelu_parts(value):
    tangent = jnp.tanh(tanh_scale * (value + 0.044715 * value * value * value))
    result = 0.5 * value * (1.0 + tangent)
    slope = 0.5 * (1.0 + tangent) + 0.5 * value * (1.0 - tangent * tangent) * tanh_scale * (1.0 + 3.0 * 0.044715 * value * value)
    return (result, slope)

def reference(tokens, up_weight, down_weight, out_grad):
    scale = 1.0 / math.sqrt(TOKENS)
    hidden = jnp.dot(tokens, up_weight, preferred_element_type=jnp.float32)
    activ, slope = gelu_parts(hidden)
    activ = activ.astype(jnp.bfloat16)
    output = jnp.dot(activ, down_weight, preferred_element_type=jnp.float32).astype(jnp.bfloat16)
    act_grad = jnp.dot(out_grad, down_weight.T, preferred_element_type=jnp.float32)
    hidden_grad = (act_grad * slope).astype(jnp.bfloat16)
    token_grad = jnp.dot(hidden_grad, up_weight.T, preferred_element_type=jnp.float32).astype(jnp.bfloat16)
    down_grad = (jnp.dot(activ.T, out_grad, preferred_element_type=jnp.float32) * scale).astype(jnp.bfloat16)
    up_grad = (jnp.dot(tokens.T, hidden_grad, preferred_element_type=jnp.float32) * scale).astype(jnp.bfloat16)
    return (output, token_grad, up_grad, down_grad)
```

```python
import math

import jax
import jax.numpy as jnp
from jax import lax
from jax.sharding import PartitionSpec as P

bf16, f32 = jnp.bfloat16, jnp.float32
tanh_scale = math.sqrt(2.0 / math.pi)

Z, XL, Y, XH, CORE = 8, 2, 4, 2, 2


def gelu_parts(value):
    tangent = jnp.tanh(tanh_scale * (value + 0.044715 * value * value * value))
    result = 0.5 * value * (1.0 + tangent)
    slope = 0.5 * (1.0 + tangent) + 0.5 * value * (1.0 - tangent * tangent) * tanh_scale * (
        1.0 + 3.0 * 0.044715 * value * value
    )
    return (result, slope)


def contract_rows(left, right):
    return lax.dot_general(
        left, right, (((0,), (0,)), ((), ())), preferred_element_type=f32
    )


def contract_cols(left, right):
    return lax.dot_general(
        left, right, (((1,), (1,)), ((), ())), preferred_element_type=f32
    )


def from_z(x, d):
    return lax.ppermute(
        x, "row", [(((z + d) % Z) * XL + k, z * XL + k) for z in range(Z) for k in range(XL)]
    )


def swap_xl(x):
    return lax.ppermute(x, "row", [(i ^ 1, i) for i in range(Z * XL)])


def from_y(x, d):
    n = XH * CORE
    return lax.ppermute(
        x, "col", [(((y + d) % Y) * n + k, y * n + k) for y in range(Y) for k in range(n)]
    )


def swap_xh(x):
    return lax.ppermute(x, "col", [(i ^ 2, i) for i in range(Y * XH * CORE)])


def swap_core(x):
    return lax.ppermute(x, "col", [(i ^ 1, i) for i in range(Y * XH * CORE)])


def gather_col(x):
    x = jnp.concatenate([x] + [from_y(x, d) for d in range(1, Y)], axis=0)
    x = jnp.concatenate([x, swap_xh(x)], axis=0)
    return jnp.concatenate([x, swap_core(x)], axis=0)


def scatter_col(x):
    n = x.shape[0] // 2
    x = x[:n] + swap_core(x[n:])
    n = n // 2
    x = x[:n] + swap_xh(x[n:].astype(bf16)).astype(f32)
    n = n // Y
    total = x[:n]
    for d in range(1, Y):
        total = total + from_y(x[d * n : (d + 1) * n], -d)
    return total.astype(bf16)


def block_of(x, r):
    n = x.shape[0] // Z
    at = lax.rem(lax.axis_index("row") // XL + r, Z) * n
    return lax.dynamic_slice_in_dim(x, at, n, axis=0)


def scatter_row(x):
    h, m = Z // 2, x.shape[1] // 2
    far = block_of(x, h)
    up = from_z(far[:, :m].astype(bf16), -1).astype(f32)
    dn = from_z(far[:, m:].astype(bf16), 1).astype(f32)
    up = block_of(x, h - 1) + lax.pad(up, 0.0, ((0, 0, 0), (0, m, 0)))
    dn = block_of(x, h + 1) + lax.pad(dn, 0.0, ((0, 0, 0), (m, 0, 0)))
    for s in range(h - 1, 0, -1):
        up = from_z(up.astype(bf16), -1).astype(f32)
        dn = from_z(dn.astype(bf16), 1).astype(f32)
        if s > 1:
            up = block_of(x, s - 1) + up
            dn = block_of(x, Z - s + 1) + dn
    total = block_of(x, 0) + up + dn
    return total + swap_xl(total.astype(bf16)).astype(f32)


def gather_row(own):
    n, cols = own.shape
    m, h = cols // 2, Z // 2
    z = lax.axis_index("row") // XL
    panel = jnp.zeros((Z * n, cols), own.dtype)

    def put(panel, piece, r, col=0):
        return lax.dynamic_update_slice(panel, piece, (lax.rem(z + r, Z) * n, col))

    panel = put(panel, own, 0)
    up, dn = own, own
    for s in range(1, h):
        up, dn = from_z(up, -1), from_z(dn, 1)
        panel = put(panel, up, Z - s)
        panel = put(panel, dn, s)
    panel = put(panel, from_z(up[:, :m], -1), h)
    return put(panel, from_z(dn[:, m:], 1), h, m)


def local(tokens, up_weight, down_weight, out_grad):
    total = tokens.shape[0] * Y * XH * CORE
    scale = 1.0 / math.sqrt(total)
    token_panel = gather_col(tokens)
    grad_panel = gather_col(out_grad)
    hidden = scatter_row(jnp.dot(token_panel, up_weight, preferred_element_type=f32))
    act_grad = scatter_row(contract_cols(grad_panel, down_weight))
    activ, slope = gelu_parts(hidden)
    act_panel = gather_row(activ.astype(bf16))
    dh_panel = gather_row((act_grad * slope).astype(bf16))
    output = scatter_col(jnp.dot(act_panel, down_weight, preferred_element_type=f32))
    token_grad = scatter_col(contract_cols(dh_panel, up_weight))
    down_grad = (contract_rows(act_panel, grad_panel) * scale).astype(bf16)
    up_grad = (contract_rows(token_panel, dh_panel) * scale).astype(bf16)
    return (output, token_grad, up_grad, down_grad)


def solution(mesh):
    placed = (P("col", "row"), P("row", "col"), P("col", "row"), P("col", "row"))
    return jax.shard_map(
        local,
        mesh=mesh,
        in_specs=placed,
        out_specs=(P("col", "row"), P("col", "row"), P("row", "col"), P("col", "row")),
        check_vma=False,
    )
```

```python
import math

import jax
import jax.numpy as jnp
from jax import lax
from jax.sharding import PartitionSpec as P

bf16, f32 = jnp.bfloat16, jnp.float32
tanh_scale = math.sqrt(2.0 / math.pi)

Z, XL, Y, XH, CORE = 8, 2, 4, 2, 2


def gelu_parts(value):
    tangent = jnp.tanh(tanh_scale * (value + 0.044715 * value * value * value))
    result = 0.5 * value * (1.0 + tangent)
    slope = 0.5 * (1.0 + tangent) + 0.5 * value * (1.0 - tangent * tangent) * tanh_scale * (
        1.0 + 3.0 * 0.044715 * value * value
    )
    return (result, slope)


def contract_rows(left, right):
    return lax.dot_general(
        left, right, (((0,), (0,)), ((), ())), preferred_element_type=f32
    )


def contract_cols(left, right):
    return lax.dot_general(
        left, right, (((1,), (1,)), ((), ())), preferred_element_type=f32
    )


def even(i, n):
    return i ^ 1


def odd(i, n):
    return (i + 1) % n if i % 2 else (i - 1) % n


def swap_z(x, pairs):
    return lax.ppermute(
        x, "row", [(pairs(z, Z) * XL + k, z * XL + k) for z in range(Z) for k in range(XL)]
    )


def swap_xl(x):
    return lax.ppermute(x, "row", [(i ^ 1, i) for i in range(Z * XL)])


def exchange_col(x):
    n = Y * XH
    groups = [[k * CORE + c for k in range(n)] for c in range(CORE)]
    return lax.all_to_all(x, "col", 0, 0, axis_index_groups=groups, tiled=True)


def swap_core(x):
    return lax.ppermute(x, "col", [(i ^ 1, i) for i in range(Y * XH * CORE)])


def gather_col(x):
    n = Y * XH
    x = jnp.broadcast_to(x[None], (n,) + x.shape).reshape(n * x.shape[0], x.shape[1])
    x = exchange_col(x)
    return jnp.concatenate([x, swap_core(x)], axis=0)


def scatter_col(x):
    n = x.shape[0] // 2
    x = x[:n] + swap_core(x[n:])
    x = exchange_col(x.astype(bf16)).astype(f32)
    return jnp.sum(x.reshape(Y * XH, -1, x.shape[1]), axis=0).astype(bf16)


def block_at(r, n):
    z = lax.axis_index("row") // XL
    return lax.rem(z + r * (1 - 2 * lax.rem(z, 2)) + Z, Z) * n


def scatter_row(x):
    n, m, h = x.shape[0] // Z, x.shape[1] // 2, Z // 2

    def block(r):
        return lax.dynamic_slice_in_dim(x, block_at(r, n), n, axis=0)

    far = block(h)
    ways = (even, odd)
    one = swap_z(far[:, :m].astype(bf16), ways[0]).astype(f32)
    two = swap_z(far[:, m:].astype(bf16), ways[1]).astype(f32)
    one = lax.pad(one, 0.0, ((0, 0, 0), (0, m, 0)))
    two = lax.pad(two, 0.0, ((0, 0, 0), (m, 0, 0)))
    sign = 1
    for s in range(h - 1, 0, -1):
        ways, sign = ways[::-1], -sign
        one = swap_z((block(sign * s) + one).astype(bf16), ways[0])
        two = swap_z((block(-sign * s) + two).astype(bf16), ways[1])
        one, two = lax.optimization_barrier((one, two))
        one, two = one.astype(f32), two.astype(f32)
    total = block(0) + one + two
    return total + swap_xl(total.astype(bf16)).astype(f32)


def gather_row(own):
    n, cols = own.shape
    m, h = cols // 2, Z // 2
    panel = jnp.zeros((Z * n, cols), own.dtype)

    def put(panel, piece, r, col=0):
        return lax.dynamic_update_slice(panel, piece, (block_at(r, n), col))

    panel = put(panel, own, 0)
    one, two = own, own
    ways, sign = (even, odd), 1
    for s in range(1, h):
        one, two = swap_z(one, ways[0]), swap_z(two, ways[1])
        panel = put(panel, one, sign * s)
        panel = put(panel, two, -sign * s)
        ways, sign = ways[::-1], -sign
    panel = put(panel, swap_z(one[:, :m], ways[0]), h)
    return put(panel, swap_z(two[:, m:], ways[1]), h, m)


def local(tokens, up_weight, down_weight, out_grad):
    total = tokens.shape[0] * Y * XH * CORE
    scale = 1.0 / math.sqrt(total)
    width = tokens.shape[1]
    panel = gather_col(jnp.concatenate([tokens, out_grad], axis=1))
    token_panel, grad_panel = panel[:, :width], panel[:, width:]
    hidden = scatter_row(jnp.dot(token_panel, up_weight, preferred_element_type=f32))
    act_grad = scatter_row(contract_cols(grad_panel, down_weight))
    activ, slope = gelu_parts(hidden)
    act_panel = gather_row(activ.astype(bf16))
    dh_panel = gather_row((act_grad * slope).astype(bf16))
    output = jnp.dot(act_panel, down_weight, preferred_element_type=f32)
    token_grad = contract_cols(dh_panel, up_weight)
    both = scatter_col(jnp.concatenate([output, token_grad], axis=1))
    down_grad = (contract_rows(act_panel, grad_panel) * scale).astype(bf16)
    up_grad = (contract_rows(token_panel, dh_panel) * scale).astype(bf16)
    return (both[:, :width], both[:, width:], up_grad, down_grad)


def solution(mesh):
    placed = (P("col", "row"), P("row", "col"), P("col", "row"), P("col", "row"))
    return jax.shard_map(
        local,
        mesh=mesh,
        in_specs=placed,
        out_specs=(P("col", "row"), P("col", "row"), P("row", "col"), P("col", "row")),
        check_vma=False,
    )
```

```python
import math

import jax
import jax.numpy as jnp
from jax import lax
from jax.sharding import PartitionSpec as P

bf16, f32 = jnp.bfloat16, jnp.float32
tanh_scale = math.sqrt(2.0 / math.pi)

Z, XL, Y, XH, CORE = 8, 2, 4, 2, 2


def gelu_parts(value):
    tangent = jnp.tanh(tanh_scale * (value + 0.044715 * value * value * value))
    result = 0.5 * value * (1.0 + tangent)
    slope = 0.5 * (1.0 + tangent) + 0.5 * value * (1.0 - tangent * tangent) * tanh_scale * (
        1.0 + 3.0 * 0.044715 * value * value
    )
    return (result, slope)


def contract_rows(left, right):
    return lax.dot_general(
        left, right, (((0,), (0,)), ((), ())), preferred_element_type=f32
    )


def contract_cols(left, right):
    return lax.dot_general(
        left, right, (((1,), (1,)), ((), ())), preferred_element_type=f32
    )


def even(i, n):
    return i ^ 1


def odd(i, n):
    return (i + 1) % n if i % 2 else (i - 1) % n


def swap_z(x, pairs):
    return lax.ppermute(
        x, "row", [(pairs(z, Z) * XL + k, z * XL + k) for z in range(Z) for k in range(XL)]
    )


def swap_xl(x):
    return lax.ppermute(x, "row", [(i ^ 1, i) for i in range(Z * XL)])


def exchange_col(x):
    n = Y * XH
    groups = [[k * CORE + c for k in range(n)] for c in range(CORE)]
    return lax.all_to_all(x, "col", 0, 0, axis_index_groups=groups, tiled=True)


def swap_core(x):
    return lax.ppermute(x, "col", [(i ^ 1, i) for i in range(Y * XH * CORE)])


def gather_col(x):
    n = Y * XH
    x = jnp.broadcast_to(x[None], (n,) + x.shape).reshape(n * x.shape[0], x.shape[1])
    x = exchange_col(x)
    return jnp.concatenate([x, swap_core(x)], axis=0)


def add_core(x):
    n = x.shape[0] // 2
    return (x[:n] + swap_core(x[n:])).astype(bf16)


def scatter_col(x):
    x = exchange_col(x).astype(f32)
    return jnp.sum(x.reshape(Y * XH, -1, x.shape[1]), axis=0).astype(bf16)


def block_at(r, n):
    z = lax.axis_index("row") // XL
    return lax.rem(z + r * (1 - 2 * lax.rem(z, 2)) + Z, Z) * n


def scatter_row(x):
    n, m, h = x.shape[0] // Z, x.shape[1] // 2, Z // 2

    def block(r):
        return lax.dynamic_slice_in_dim(x, block_at(r, n), n, axis=0)

    far = block(h)
    ways = (even, odd)
    one = swap_z(far[:, :m].astype(bf16), ways[0]).astype(f32)
    two = swap_z(far[:, m:].astype(bf16), ways[1]).astype(f32)
    one = lax.pad(one, 0.0, ((0, 0, 0), (0, m, 0)))
    two = lax.pad(two, 0.0, ((0, 0, 0), (m, 0, 0)))
    sign = 1
    for s in range(h - 1, 0, -1):
        ways, sign = ways[::-1], -sign
        one = swap_z((block(sign * s) + one).astype(bf16), ways[0])
        two = swap_z((block(-sign * s) + two).astype(bf16), ways[1])
        one, two = lax.optimization_barrier((one, two))
        one, two = one.astype(f32), two.astype(f32)
    total = block(0) + one + two
    return total + swap_xl(total.astype(bf16)).astype(f32)


def gather_row(own):
    n, cols = own.shape
    m, h = cols // 2, Z // 2
    panel = jnp.zeros((Z * n, cols), own.dtype)

    def put(panel, piece, r, col=0):
        return lax.dynamic_update_slice(panel, piece, (block_at(r, n), col))

    panel = put(panel, own, 0)
    one, two = own, own
    ways, sign = (even, odd), 1
    for s in range(1, h):
        one, two = swap_z(one, ways[0]), swap_z(two, ways[1])
        panel = put(panel, one, sign * s)
        panel = put(panel, two, -sign * s)
        ways, sign = ways[::-1], -sign
    panel = put(panel, swap_z(one[:, :m], ways[0]), h)
    return put(panel, swap_z(two[:, m:], ways[1]), h, m)


def local(tokens, up_weight, down_weight, out_grad):
    total = tokens.shape[0] * Y * XH * CORE
    scale = 1.0 / math.sqrt(total)
    width = tokens.shape[1]
    panel = gather_col(jnp.concatenate([tokens, out_grad], axis=1))
    token_panel, grad_panel = panel[:, :width], panel[:, width:]
    hidden = scatter_row(jnp.dot(token_panel, up_weight, preferred_element_type=f32))
    act_grad = scatter_row(contract_cols(grad_panel, down_weight))
    activ, slope = gelu_parts(hidden)
    act_panel = gather_row(activ.astype(bf16))
    dh_panel = gather_row((act_grad * slope).astype(bf16))
    output = add_core(jnp.dot(act_panel, down_weight, preferred_element_type=f32))
    token_grad = add_core(contract_cols(dh_panel, up_weight))
    both = scatter_col(jnp.concatenate([output, token_grad], axis=1))
    down_grad = (contract_rows(act_panel, grad_panel) * scale).astype(bf16)
    up_grad = (contract_rows(token_panel, dh_panel) * scale).astype(bf16)
    return (both[:, :width], both[:, width:], up_grad, down_grad)


def solution(mesh):
    placed = (P("col", "row"), P("row", "col"), P("col", "row"), P("col", "row"))
    return jax.shard_map(
        local,
        mesh=mesh,
        in_specs=placed,
        out_specs=(P("col", "row"), P("col", "row"), P("row", "col"), P("col", "row")),
        check_vma=False,
    )
```

```python
import math

import jax
import jax.numpy as jnp
from jax import lax
from jax.sharding import PartitionSpec as P

bf16, f32 = jnp.bfloat16, jnp.float32
tanh_scale = math.sqrt(2.0 / math.pi)

Z, XL, Y, XH, CORE = 8, 2, 4, 2, 2


def gelu_parts(value):
    tangent = jnp.tanh(tanh_scale * (value + 0.044715 * value * value * value))
    result = 0.5 * value * (1.0 + tangent)
    slope = 0.5 * (1.0 + tangent) + 0.5 * value * (1.0 - tangent * tangent) * tanh_scale * (
        1.0 + 3.0 * 0.044715 * value * value
    )
    return (result, slope)


def contract_rows(left, right):
    return lax.dot_general(
        left, right, (((0,), (0,)), ((), ())), preferred_element_type=f32
    )


def contract_cols(left, right):
    return lax.dot_general(
        left, right, (((1,), (1,)), ((), ())), preferred_element_type=f32
    )


def even(i, n):
    return i ^ 1


def odd(i, n):
    return (i + 1) % n if i % 2 else (i - 1) % n


def swap_z(x, pairs):
    return lax.ppermute(
        x, "row", [(pairs(z, Z) * XL + k, z * XL + k) for z in range(Z) for k in range(XL)]
    )


def swap_xl(x):
    return lax.ppermute(x, "row", [(i ^ 1, i) for i in range(Z * XL)])


def exchange_col(x):
    n = Y * XH
    groups = [[k * CORE + c for k in range(n)] for c in range(CORE)]
    return lax.all_to_all(x, "col", 0, 0, axis_index_groups=groups, tiled=True)


def swap_core(x):
    return lax.ppermute(x, "col", [(i ^ 1, i) for i in range(Y * XH * CORE)])


def gather_col(x):
    n = Y * XH
    x = jnp.broadcast_to(x[None], (n,) + x.shape).reshape(n * x.shape[0], x.shape[1])
    x = exchange_col(x)
    m = x.shape[1] // 2
    return [jnp.concatenate([y, swap_core(y)], axis=0) for y in (x[:, :m], x[:, m:])]


def add_core(x):
    n = x.shape[0] // 2
    return (x[:n] + swap_core(x[n:])).astype(bf16)


def scatter_col(x):
    x = exchange_col(x).astype(f32)
    return jnp.sum(x.reshape(Y * XH, -1, x.shape[1]), axis=0).astype(bf16)


def block_at(r, n):
    z = lax.axis_index("row") // XL
    return lax.rem(z + r * (1 - 2 * lax.rem(z, 2)) + Z, Z) * n


def scatter_row(x):
    n, m, h = x.shape[0] // Z, x.shape[1] // 2, Z // 2

    def block(r):
        return lax.dynamic_slice_in_dim(x, block_at(r, n), n, axis=0)

    far = block(h)
    ways = (even, odd)
    one = swap_z(far[:, :m].astype(bf16), ways[0]).astype(f32)
    two = swap_z(far[:, m:].astype(bf16), ways[1]).astype(f32)
    one = lax.pad(one, 0.0, ((0, 0, 0), (0, m, 0)))
    two = lax.pad(two, 0.0, ((0, 0, 0), (m, 0, 0)))
    sign = 1
    for s in range(h - 1, 0, -1):
        ways, sign = ways[::-1], -sign
        one = swap_z((block(sign * s) + one).astype(bf16), ways[0])
        two = swap_z((block(-sign * s) + two).astype(bf16), ways[1])
        one, two = lax.optimization_barrier((one, two))
        one, two = one.astype(f32), two.astype(f32)
    total = block(0) + one + two
    return total + swap_xl(total.astype(bf16)).astype(f32)


def gather_row(own):
    n, cols = own.shape
    m, h = cols // 2, Z // 2
    panel = jnp.zeros((Z * n, cols), own.dtype)

    def put(panel, piece, r, col=0):
        return lax.dynamic_update_slice(panel, piece, (block_at(r, n), col))

    panel = put(panel, own, 0)
    one, two = own, own
    ways, sign = (even, odd), 1
    for s in range(1, h):
        one, two = swap_z(one, ways[0]), swap_z(two, ways[1])
        panel = put(panel, one, sign * s)
        panel = put(panel, two, -sign * s)
        ways, sign = ways[::-1], -sign
    panel = put(panel, swap_z(one[:, :m], ways[0]), h)
    return put(panel, swap_z(two[:, m:], ways[1]), h, m)


def local(tokens, up_weight, down_weight, out_grad):
    total = tokens.shape[0] * Y * XH * CORE
    scale = 1.0 / math.sqrt(total)
    width = tokens.shape[1]
    token_panel, grad_panel = gather_col(jnp.concatenate([tokens, out_grad], axis=1))
    hidden = scatter_row(jnp.dot(token_panel, up_weight, preferred_element_type=f32))
    act_grad = scatter_row(contract_cols(grad_panel, down_weight))
    activ, slope = gelu_parts(hidden)
    act_panel = gather_row(activ.astype(bf16))
    dh_panel = gather_row((act_grad * slope).astype(bf16))
    output = add_core(jnp.dot(act_panel, down_weight, preferred_element_type=f32))
    token_grad = add_core(contract_cols(dh_panel, up_weight))
    both = scatter_col(jnp.concatenate([output, token_grad], axis=1))
    down_grad = (contract_rows(act_panel, grad_panel) * scale).astype(bf16)
    up_grad = (contract_rows(token_panel, dh_panel) * scale).astype(bf16)
    return (both[:, :width], both[:, width:], up_grad, down_grad)


def solution(mesh):
    placed = (P("col", "row"), P("row", "col"), P("col", "row"), P("col", "row"))
    return jax.shard_map(
        local,
        mesh=mesh,
        in_specs=placed,
        out_specs=(P("col", "row"), P("col", "row"), P("row", "col"), P("col", "row")),
        check_vma=False,
    )
```

```python
import math

import jax
import jax.numpy as jnp
from jax import lax
from jax.sharding import PartitionSpec as P

bf16, f32 = jnp.bfloat16, jnp.float32
tanh_scale = math.sqrt(2.0 / math.pi)

Z, XL, Y, XH, CORE = 8, 2, 4, 2, 2


def gelu_parts(value):
    tangent = jnp.tanh(tanh_scale * (value + 0.044715 * value * value * value))
    result = 0.5 * value * (1.0 + tangent)
    slope = 0.5 * (1.0 + tangent) + 0.5 * value * (1.0 - tangent * tangent) * tanh_scale * (
        1.0 + 3.0 * 0.044715 * value * value
    )
    return (result, slope)


def contract_rows(left, right):
    return lax.dot_general(
        left, right, (((0,), (0,)), ((), ())), preferred_element_type=f32
    )


def contract_cols(left, right):
    return lax.dot_general(
        left, right, (((1,), (1,)), ((), ())), preferred_element_type=f32
    )


def even(i, n):
    return i ^ 1


def odd(i, n):
    return (i + 1) % n if i % 2 else (i - 1) % n


def swap_z(x, pairs):
    return lax.ppermute(
        x, "row", [(pairs(z, Z) * XL + k, z * XL + k) for z in range(Z) for k in range(XL)]
    )


def swap_xl(x):
    return lax.ppermute(x, "row", [(i ^ 1, i) for i in range(Z * XL)])


def exchange_col(x):
    n = Y * XH
    groups = [[k * CORE + c for k in range(n)] for c in range(CORE)]
    return lax.all_to_all(x, "col", 0, 0, axis_index_groups=groups, tiled=True)


def swap_core(x):
    return lax.ppermute(x, "col", [(i ^ 1, i) for i in range(Y * XH * CORE)])


def gather_col(x):
    n = Y * XH
    x = jnp.broadcast_to(x[None], (n,) + x.shape).reshape(n * x.shape[0], x.shape[1])
    x = exchange_col(x)
    m = x.shape[1] // 2
    return [jnp.concatenate([y, swap_core(y)], axis=0) for y in (x[:, :m], x[:, m:])]


def add_core(product, x):
    n = x.shape[0] // 2
    away = swap_core(product(x[n:]))
    own = lax.optimization_barrier(product(x[:n]))
    return (own + away).astype(bf16)


def scatter_col(x):
    x = exchange_col(x).astype(f32)
    return jnp.sum(x.reshape(Y * XH, -1, x.shape[1]), axis=0).astype(bf16)


def block_at(r, n):
    z = lax.axis_index("row") // XL
    return lax.rem(z + r * (1 - 2 * lax.rem(z, 2)) + Z, Z) * n


def scatter_row(x):
    n, m, h = x.shape[0] // Z, x.shape[1] // 2, Z // 2

    def block(r):
        return lax.dynamic_slice_in_dim(x, block_at(r, n), n, axis=0)

    far = block(h)
    ways = (even, odd)
    one = swap_z(far[:, :m].astype(bf16), ways[0]).astype(f32)
    two = swap_z(far[:, m:].astype(bf16), ways[1]).astype(f32)
    one = lax.pad(one, 0.0, ((0, 0, 0), (0, m, 0)))
    two = lax.pad(two, 0.0, ((0, 0, 0), (m, 0, 0)))
    sign = 1
    for s in range(h - 1, 0, -1):
        ways, sign = ways[::-1], -sign
        one = swap_z((block(sign * s) + one).astype(bf16), ways[0])
        two = swap_z((block(-sign * s) + two).astype(bf16), ways[1])
        one, two = lax.optimization_barrier((one, two))
        one, two = one.astype(f32), two.astype(f32)
    total = block(0) + one + two
    return total + swap_xl(total.astype(bf16)).astype(f32)


def gather_row(own):
    n, cols = own.shape
    m, h = cols // 2, Z // 2
    panel = jnp.zeros((Z * n, cols), own.dtype)

    def put(panel, piece, r, col=0):
        return lax.dynamic_update_slice(panel, piece, (block_at(r, n), col))

    panel = put(panel, own, 0)
    one, two = own, own
    ways, sign = (even, odd), 1
    for s in range(1, h):
        one, two = swap_z(one, ways[0]), swap_z(two, ways[1])
        panel = put(panel, one, sign * s)
        panel = put(panel, two, -sign * s)
        ways, sign = ways[::-1], -sign
    panel = put(panel, swap_z(one[:, :m], ways[0]), h)
    return put(panel, swap_z(two[:, m:], ways[1]), h, m)


def local(tokens, up_weight, down_weight, out_grad):
    total = tokens.shape[0] * Y * XH * CORE
    scale = 1.0 / math.sqrt(total)
    token_panel, grad_panel = gather_col(jnp.concatenate([tokens, out_grad], axis=1))
    hidden = scatter_row(jnp.dot(token_panel, up_weight, preferred_element_type=f32))
    act_grad = scatter_row(contract_cols(grad_panel, down_weight))
    activ, slope = gelu_parts(hidden)
    act_panel = gather_row(activ.astype(bf16))
    dh_panel = gather_row((act_grad * slope).astype(bf16))
    output = add_core(lambda x: jnp.dot(x, down_weight, preferred_element_type=f32), act_panel)
    token_grad = add_core(lambda x: contract_cols(x, up_weight), dh_panel)
    both = scatter_col(jnp.concatenate([output, token_grad], axis=1))
    width = tokens.shape[1]
    down_grad = (contract_rows(act_panel, grad_panel) * scale).astype(bf16)
    up_grad = (contract_rows(token_panel, dh_panel) * scale).astype(bf16)
    return (both[:, :width], both[:, width:], up_grad, down_grad)


def solution(mesh):
    placed = (P("col", "row"), P("row", "col"), P("col", "row"), P("col", "row"))
    return jax.shard_map(
        local,
        mesh=mesh,
        in_specs=placed,
        out_specs=(P("col", "row"), P("col", "row"), P("row", "col"), P("col", "row")),
        check_vma=False,
    )
```

```python
import math

import jax
import jax.numpy as jnp
from jax import lax
from jax.sharding import PartitionSpec as P

bf16, f32 = jnp.bfloat16, jnp.float32
tanh_scale = math.sqrt(2.0 / math.pi)

Z, XL, Y, XH, CORE = 8, 2, 4, 2, 2


def gelu_parts(value):
    tangent = jnp.tanh(tanh_scale * (value + 0.044715 * value * value * value))
    result = 0.5 * value * (1.0 + tangent)
    slope = 0.5 * (1.0 + tangent) + 0.5 * value * (1.0 - tangent * tangent) * tanh_scale * (
        1.0 + 3.0 * 0.044715 * value * value
    )
    return (result, slope)


def contract_rows(left, right):
    return lax.dot_general(
        left, right, (((0,), (0,)), ((), ())), preferred_element_type=f32
    )


def contract_cols(left, right):
    return lax.dot_general(
        left, right, (((1,), (1,)), ((), ())), preferred_element_type=f32
    )


def even(i, n):
    return i ^ 1


def odd(i, n):
    return (i + 1) % n if i % 2 else (i - 1) % n


def swap_z(x, pairs):
    return lax.ppermute(
        x, "row", [(pairs(z, Z) * XL + k, z * XL + k) for z in range(Z) for k in range(XL)]
    )


def swap_xl(x):
    return lax.ppermute(x, "row", [(i ^ 1, i) for i in range(Z * XL)])


def exchange_col(x):
    n = Y * XH
    groups = [[k * CORE + c for k in range(n)] for c in range(CORE)]
    return lax.all_to_all(x, "col", 0, 0, axis_index_groups=groups, tiled=True)


def swap_core(x):
    return lax.ppermute(x, "col", [(i ^ 1, i) for i in range(Y * XH * CORE)])


def gather_col(x):
    n = Y * XH
    x = jnp.broadcast_to(x[None], (n,) + x.shape).reshape(n * x.shape[0], x.shape[1])
    x = exchange_col(x)
    m = x.shape[1] // 2
    first, second = x[:, :m], x[:, m:]
    first = jnp.concatenate([first, swap_core(first)], axis=0)
    first, second = lax.optimization_barrier((first, second))
    return first, jnp.concatenate([second, swap_core(second)], axis=0)


def add_core(product, x):
    n = x.shape[0] // 2
    away = swap_core(product(x[n:]))
    own = lax.optimization_barrier(product(x[:n]))
    return (own + away).astype(bf16)


def scatter_col(x):
    x = exchange_col(x)
    x = x.reshape(Y * XH, -1, x.shape[1])
    m = x.shape[2] // 2
    sums = []
    for y in (x[:, :, :m], x[:, :, m:]):
        total = y[0].astype(f32)
        for k in range(1, Y * XH):
            total = total + y[k].astype(f32)
        sums.append(total.astype(bf16))
    return sums


def block_at(r, n):
    z = lax.axis_index("row") // XL
    return lax.rem(z + r * (1 - 2 * lax.rem(z, 2)) + Z, Z) * n


def scatter_row(x):
    n, m, h = x.shape[0] // Z, x.shape[1] // 2, Z // 2

    def block(r):
        return lax.dynamic_slice_in_dim(x, block_at(r, n), n, axis=0)

    far = block(h)
    ways = (even, odd)
    one = swap_z(far[:, :m].astype(bf16), ways[0]).astype(f32)
    two = swap_z(far[:, m:].astype(bf16), ways[1]).astype(f32)
    one = lax.pad(one, 0.0, ((0, 0, 0), (0, m, 0)))
    two = lax.pad(two, 0.0, ((0, 0, 0), (m, 0, 0)))
    sign = 1
    for s in range(h - 1, 0, -1):
        ways, sign = ways[::-1], -sign
        one = swap_z((block(sign * s) + one).astype(bf16), ways[0])
        two = swap_z((block(-sign * s) + two).astype(bf16), ways[1])
        one, two = lax.optimization_barrier((one, two))
        one, two = one.astype(f32), two.astype(f32)
    total = block(0) + one + two
    return total + swap_xl(total.astype(bf16)).astype(f32)


def gather_row(own):
    n, cols = own.shape
    m, h = cols // 2, Z // 2
    panel = jnp.zeros((Z * n, cols), own.dtype)

    def put(panel, piece, r, col=0):
        return lax.dynamic_update_slice(panel, piece, (block_at(r, n), col))

    panel = put(panel, own, 0)
    one, two = own, own
    ways, sign = (even, odd), 1
    for s in range(1, h):
        one, two = swap_z(one, ways[0]), swap_z(two, ways[1])
        panel = put(panel, one, sign * s)
        panel = put(panel, two, -sign * s)
        ways, sign = ways[::-1], -sign
    panel = put(panel, swap_z(one[:, :m], ways[0]), h)
    return put(panel, swap_z(two[:, m:], ways[1]), h, m)


def local(tokens, up_weight, down_weight, out_grad):
    total = tokens.shape[0] * Y * XH * CORE
    scale = 1.0 / math.sqrt(total)
    token_panel, grad_panel = gather_col(jnp.concatenate([tokens, out_grad], axis=1))
    hidden = scatter_row(jnp.dot(token_panel, up_weight, preferred_element_type=f32))
    act_grad = scatter_row(contract_cols(grad_panel, down_weight))
    activ, slope = gelu_parts(hidden)
    act_panel = gather_row(activ.astype(bf16))
    dh_panel = gather_row((act_grad * slope).astype(bf16))
    output = add_core(lambda x: jnp.dot(x, down_weight, preferred_element_type=f32), act_panel)
    token_grad = add_core(lambda x: contract_cols(x, up_weight), dh_panel)
    output, token_grad = scatter_col(jnp.concatenate([output, token_grad], axis=1))
    down_grad = (contract_rows(act_panel, grad_panel) * scale).astype(bf16)
    up_grad = (contract_rows(token_panel, dh_panel) * scale).astype(bf16)
    return (output, token_grad, up_grad, down_grad)


def solution(mesh):
    placed = (P("col", "row"), P("row", "col"), P("col", "row"), P("col", "row"))
    return jax.shard_map(
        local,
        mesh=mesh,
        in_specs=placed,
        out_specs=(P("col", "row"), P("col", "row"), P("row", "col"), P("col", "row")),
        check_vma=False,
    )
```
